32 devices in a mesh: dp: 8 (over z, core), tensor: 4 (over y, x).
Axes of the slice: x: 2, y: 2, z: 4, core: 2. Of those that a mesh axis runs over, the one named last changes fastest.
Arguments:
- hidden_input: bfloat16 [8192, 8192], P('dp', 'tensor'), may hold values from -6 to 6
- key_value_weight: bfloat16 [8192, 2048], P('tensor'), may hold values from -0.0625 to 0.0625
- adapter_down_weight: bfloat16 [128, 8192, 128], P('dp', 'tensor'), may hold values from -0.0625 to 0.0625
- adapter_up_weight: bfloat16 [128, 64, 2048], P('dp', None, 'tensor'), may hold values from -0.75 to 0.75
- queries: bfloat16 [8, 8192, 8, 128], P('tensor', 'dp'), may hold values from -12 to 12
- key_value_cache: bfloat16 [2, 8, 8192, 32, 128], P(None, 'tensor', 'dp'), may hold values from -12 to 12
- request_adapter_index: int32 [8192], P('dp'), may hold values from 0 to 127, as said below
- cached_length: int32 [8192], P('dp'), may hold values from 2 to 32
Outputs:
- new_kv: bfloat16 [2, 8, 8192, 128], P(None, 'tensor', 'dp')
- attn_out: bfloat16 [8, 8192, 8, 128], P('tensor', 'dp')
The draws below stay inside these ranges and needn't reach their ends.
Inputs may be any that keep to these rules, and one draw needn't show every extreme that they name: Write owner(r) = request_adapter_index[r] // 16. In each block of 1024 requests (those of one index of dp) owner(r) never falls from one request to the next; at most 256 requests of a block name one owner, and one owner is named by exactly 256 requests of every block.
All inputs are finite; a program needn't handle non-finite values.
Results may differ from the reference program's by a relative error of at most 0.009.
Values may be sent and summed in bfloat16 or wider, within the bound.
A program may use at most 192 MiB of HBM per device.

```python
import jax
import jax.numpy as jnp
from jax import lax

MODEL_WIDTH = 8192
KEY_VALUE_HEADS = 8
HEAD_WIDTH = 128
GROUP = 8
ADAPTER_RANK = 64
ADP_DEV = 16
REQ_DEV = 1024
CTX = 32
ADAPTER_TOTAL = 128
REQUESTS = 8192
SPLIT = 1
CAP = 256
N_DP = 8


def draw_queries(key, part):
    full_shape = (KEY_VALUE_HEADS * SPLIT, REQUESTS // SPLIT, GROUP, HEAD_WIDTH)
    values = jax.random.truncated_normal(key, -4.0, 4.0, full_shape, jnp.float32)
    return values.astype(jnp.bfloat16)


def draw_key_value_cache(key, part):
    full_shape = (2, KEY_VALUE_HEADS * SPLIT, REQUESTS // SPLIT, CTX, HEAD_WIDTH)
    own_key = jax.random.fold_in(key, 29)
    values = jax.random.truncated_normal(own_key, -4.0, 4.0, full_shape, jnp.float32)
    return values.astype(jnp.bfloat16)


def draw_request_adapter_index(key, part):
    block_count = REQUESTS // REQ_DEV
    owner_count = ADAPTER_TOTAL // ADP_DEV
    hot_key, spread_key, local_key = jax.random.split(jax.random.fold_in(key, 41), 3)
    hot_owner = jax.random.randint(hot_key, (), 0, owner_count)
    remaining = REQ_DEV - CAP
    base_count = remaining // (owner_count - 1)
    leftover = remaining - base_count * (owner_count - 1)
    spread = jax.random.randint(spread_key, (block_count, owner_count - 1), 0, base_count + 1)
    others = base_count + spread - jnp.roll(spread, -1, axis=1) + (jnp.arange(owner_count - 1) < leftover).astype(jnp.int32)[None, :]
    owner_range = jnp.arange(owner_count)
    other_slot = jnp.clip(jnp.where(owner_range < hot_owner, owner_range, owner_range - 1), 0, owner_count - 2)
    counts = jnp.where(owner_range[None, :] == hot_owner, CAP, jnp.take(others, other_slot, axis=1))
    ends = jnp.cumsum(counts, axis=1)
    positions = jnp.arange(REQ_DEV)
    owner_of = jnp.sum((positions[None, :, None] >= ends[:, None, :]).astype(jnp.int32), axis=2)
    local_pick = jax.random.randint(local_key, (block_count, REQ_DEV), 0, ADP_DEV)
    return (owner_of * ADP_DEV + local_pick).reshape(REQUESTS).astype(jnp.int32)


def with_ends(entries, stream_key, least, high):
    longest = entries.shape.index(max(entries.shape))
    spots = []
    for shift in (0, 1):
        where = [jax.random.randint(jax.random.fold_in(stream_key, axis), (), 0, length) for axis, length in enumerate(entries.shape)]
        where[longest] = (where[longest] + shift) % entries.shape[longest]
        spots.append(tuple(where))
    return entries.at[spots[0]].set(least).at[spots[1]].set(high)


def block_scale(key, extent, shards, least, largest):
    factor_of, own = 1.0, jax.random.fold_in(key, 6)
    for axis_at, shards_of in shards:
        heights = jnp.exp(jax.random.uniform(jax.random.fold_in(own, axis_at), (shards_of,), jnp.float32, least / len(shards), largest / len(shards)))
        factor_of = factor_of * jnp.repeat(heights, extent[axis_at] // shards_of).reshape([-1 if axis == axis_at else 1 for axis in range(len(extent))])
    return factor_of


def gaussian(rng, shape, scale, reach, pieces=(), kind=jnp.bfloat16):
    drawn = jax.random.normal(rng, shape, jnp.float32) * scale
    if len(pieces) > 0:
        drawn = block_scale(rng, shape, pieces, -0.22, 0.18) * drawn
    return jnp.clip(drawn, min=-reach, max=reach).astype(kind)


def setup_inputs(seed: int = 0) -> dict:
    key_list = jax.random.split(jax.random.key(seed), 9)
    hidden_input = gaussian(key_list[0], (REQUESTS, MODEL_WIDTH), 1.0, 6.0, ((0, 8), (1, 4)))
    key_value_weight = gaussian(key_list[1], (MODEL_WIDTH, 2 * KEY_VALUE_HEADS * HEAD_WIDTH), MODEL_WIDTH ** -0.5, 0.0625, ((0, 4),))
    adapter_down_weight = gaussian(key_list[2], (ADAPTER_TOTAL, MODEL_WIDTH, 2 * ADAPTER_RANK), MODEL_WIDTH ** -0.5, 0.0625, ((0, 8), (1, 4)))
    adapter_up_weight = gaussian(key_list[3], (ADAPTER_TOTAL, ADAPTER_RANK, 2 * KEY_VALUE_HEADS * HEAD_WIDTH), ADAPTER_RANK ** -0.5, 0.75, ((0, 8), (2, 4)))
    queries = draw_queries(jax.random.fold_in(key_list[8], 71), 0)
    key_value_cache = draw_key_value_cache(jax.random.fold_in(key_list[8], 71), 0)
    request_adapter_index = draw_request_adapter_index(jax.random.fold_in(key_list[8], 71), 0)
    cached_length = with_ends(jax.random.randint(key_list[7], (REQUESTS,), 2, CTX + 1), jax.random.fold_in(key_list[7], 1), 2, CTX).astype(jnp.int32)
    return dict(hidden_input=hidden_input, key_value_weight=key_value_weight, adapter_down_weight=adapter_down_weight, adapter_up_weight=adapter_up_weight, queries=queries, key_value_cache=key_value_cache, request_adapter_index=request_adapter_index, cached_length=cached_length)


rope_theta = 500000.0

def rotate_keys(key_rows, positions):
    head_size = key_rows.shape[-1]
    half_dim = head_size // 2
    freq_index = jnp.arange(half_dim).astype(key_rows.dtype)
    inverse = rope_theta ** (-(2.0 * freq_index / head_size))
    angles = positions[..., None].astype(key_rows.dtype) * inverse
    cosine = jnp.cos(angles)
    sine_part = jnp.sin(angles)
    first_half = key_rows[..., :half_dim]
    second_half = key_rows[..., half_dim:]
    return jnp.concatenate([first_half * cosine - second_half * sine_part, second_half * cosine + first_half * sine_part], axis=-1)

def attend(query_rows, cache_keys, cache_values, new_keys, new_values, lengths):
    score_scale = 1.0 / jnp.sqrt(jnp.float32(query_rows.shape[-1]))
    query_wide = query_rows.astype(jnp.float32)
    cache_scores = jnp.einsum('igd,icd->igc', query_wide, cache_keys.astype(jnp.float32)) * score_scale
    own_scores = jnp.einsum('igd,id->ig', query_wide, new_keys.astype(jnp.float32)) * score_scale
    valid_mask = (jnp.arange(cache_keys.shape[1])[None, :] < lengths[:, None])[:, None, :]
    masked = jnp.where(valid_mask, cache_scores, -1e+30)
    peak_score = jnp.maximum(lax.optimization_barrier(jnp.max(masked, axis=-1)), own_scores)
    cache_exp = jnp.where(valid_mask, jnp.exp(masked - peak_score[..., None]), 0.0)
    own_exp = jnp.exp(own_scores - peak_score)
    denominator = lax.optimization_barrier(jnp.sum(cache_exp, axis=-1)) + own_exp
    cache_weights = (cache_exp / denominator[..., None]).astype(jnp.bfloat16)
    own_weights = (own_exp / denominator).astype(jnp.bfloat16)
    attended = jnp.einsum('igc,icd->igd', cache_weights.astype(jnp.float32), cache_values.astype(jnp.float32))
    attended = attended + own_weights.astype(jnp.float32)[..., None] * new_values.astype(jnp.float32)[:, None, :]
    return attended.astype(jnp.bfloat16)

def reference(hidden_input, key_value_weight, adapter_down_weight, adapter_up_weight, queries, key_value_cache, request_adapter_index, cached_length):
    base_kv = jnp.dot(hidden_input, key_value_weight, preferred_element_type=jnp.float32)

    def apply_block(block_pair):
        request_row_block, adapter_index_block = block_pair
        lowered_rows = adapter_down_weight[adapter_index_block].astype(jnp.float32)
        rank_mid = jnp.einsum('rd,rdk->rk', request_row_block.astype(jnp.float32), lowered_rows).astype(jnp.bfloat16)
        rank_wide = rank_mid.astype(jnp.float32)
        raised_rows = adapter_up_weight[adapter_index_block].astype(jnp.float32).reshape(request_row_block.shape[0], ADAPTER_RANK, KEY_VALUE_HEADS, 2, HEAD_WIDTH)
        key_part = jnp.einsum('ri,rihe->rhe', rank_wide[:, :ADAPTER_RANK], raised_rows[:, :, :, 0, :])
        value_part = jnp.einsum('ri,rihe->rhe', rank_wide[:, ADAPTER_RANK:], raised_rows[:, :, :, 1, :])
        delta_cols = jnp.stack([key_part, value_part], axis=2).reshape(request_row_block.shape[0], 2 * KEY_VALUE_HEADS * HEAD_WIDTH)
        return delta_cols.astype(jnp.bfloat16)
    block_count = REQUESTS // 8
    deltas = lax.map(apply_block, (hidden_input.reshape(block_count, 8, MODEL_WIDTH), request_adapter_index.reshape(block_count, 8)))
    fresh_kv = base_kv + deltas.reshape(REQUESTS, 2 * KEY_VALUE_HEADS * HEAD_WIDTH).astype(jnp.float32)
    half_rows = REQ_DEV // SPLIT
    fresh_view = fresh_kv.reshape(N_DP, SPLIT, half_rows, KEY_VALUE_HEADS, 2, HEAD_WIDTH).transpose(4, 3, 1, 0, 2, 5)
    fresh_view = fresh_view.reshape(2, KEY_VALUE_HEADS * SPLIT, N_DP * half_rows, HEAD_WIDTH)
    lens_view = cached_length.reshape(N_DP, SPLIT, half_rows).transpose(1, 0, 2).reshape(SPLIT, N_DP * half_rows)
    lens_view = jnp.tile(lens_view, (KEY_VALUE_HEADS, 1))
    new_keys = rotate_keys(fresh_view[0], lens_view)
    new_kv = jnp.stack([new_keys, fresh_view[1]]).astype(jnp.bfloat16)

    def attend_head(head_pack):
        return attend(*head_pack)
    attn_out = lax.map(attend_head, (queries, key_value_cache[0], key_value_cache[1], new_kv[0], new_kv[1], lens_view))
    return (new_kv, attn_out)
```

```python
import functools

import jax
import jax.numpy as jnp
from jax import lax
from jax.experimental import pallas as pl
from jax.experimental.pallas import tpu as pltpu
from jax.sharding import PartitionSpec as P

rope_theta = 500000.0
MESH = pl.DeviceIdType.MESH
BF = jnp.bfloat16
F32 = jnp.float32
CHUNKS = 4
BIG = -1e30


def project_kernel(
    n, m, adapters, hid, idr, idc, w_hbm, dn_hbm, up_hbm, fresh,
    wv, dv, uv, stage, recv, idsend, idrecv, idb, part, rsrecv, rkown, rkrecv, dout, ret,
    load_sem, row_s, row_r, id_s, id_r, rs_s, rs_r, rk_s, rk_r, dl_s, dl_r,
):
    me = lax.axis_index("dp")
    mt = lax.axis_index("tensor")
    rows, feats = hid.shape
    cap = stage.shape[1]
    step = cap // CHUNKS
    cols = fresh.shape[1]
    far = sorted(range(1, n), key=lambda k: (abs(k - n // 2), k))

    def dp_of(k):
        return lax.rem(me + k + n, n)

    def tp_of(k):
        return lax.rem(mt + k + m, m)

    barrier = pltpu.get_barrier_semaphore()
    for k in range(1, n):
        pl.semaphore_signal(barrier, inc=1, device_id=(dp_of(k), mt), device_id_type=MESH)
    for k in range(1, m):
        pl.semaphore_signal(barrier, inc=1, device_id=(me, tp_of(k)), device_id_type=MESH)
    loads = [
        pltpu.make_async_copy(w_hbm, wv, load_sem.at[0]),
        pltpu.make_async_copy(dn_hbm, dv, load_sem.at[1]),
        pltpu.make_async_copy(up_hbm, uv, load_sem.at[2]),
    ]
    for load in loads:
        load.start()
    pl.semaphore_wait(barrier, n - 1 + m - 1)

    def row_copy(c, k):
        return pltpu.make_async_remote_copy(
            src_ref=stage.at[k, pl.ds(pl.multiple_of(c * step, step), step)],
            dst_ref=recv.at[c, k],
            send_sem=row_s.at[c, k], recv_sem=row_r.at[c, k],
            device_id=(dp_of(k), mt), device_id_type=MESH,
        )

    def id_copy(k):
        return pltpu.make_async_remote_copy(
            src_ref=idsend.at[k], dst_ref=idrecv.at[k],
            send_sem=id_s.at[k], recv_sem=id_r.at[k],
            device_id=(dp_of(k), mt), device_id_type=MESH,
        )

    def rs_copy(k):
        return pltpu.make_async_remote_copy(
            src_ref=part.at[k], dst_ref=rsrecv.at[k],
            send_sem=rs_s.at[k], recv_sem=rs_r.at[k],
            device_id=(me, tp_of(k)), device_id_type=MESH,
        )

    def rank_copy(c, k):
        return pltpu.make_async_remote_copy(
            src_ref=rkown.at[c], dst_ref=rkrecv.at[c, k],
            send_sem=rk_s.at[c, k], recv_sem=rk_r.at[c, k],
            device_id=(me, tp_of(k)), device_id_type=MESH,
        )

    def delta_copy(c, k):
        return pltpu.make_async_remote_copy(
            src_ref=dout.at[c, k], dst_ref=ret.at[c, k],
            send_sem=dl_s.at[c, k], recv_sem=dl_r.at[c, k],
            device_id=(dp_of(-k), mt), device_id_type=MESH,
        )

    ids_row = idr[0:1, :]

    def start_of(owner):
        below = jnp.where(ids_row < owner * adapters, 1.0, 0.0)
        return jnp.minimum(jnp.sum(below, axis=1, keepdims=True), float(rows - cap))

    gap = (
        lax.broadcasted_iota(jnp.int32, (cap, rows), 1)
        - lax.broadcasted_iota(jnp.int32, (cap, rows), 0)
    ).astype(F32)
    width = 512
    for k in far + [0]:
        owner = dp_of(k)
        pick = jnp.where(gap == start_of(owner), 1.0, 0.0).astype(BF)
        local = (ids_row - owner * adapters).astype(F32)
        local = jnp.broadcast_to(local, (16, rows)).astype(BF)
        picked = lax.dot_general(
            local, pick, (((1,), (1,)), ((), ())), preferred_element_type=F32
        ).astype(BF)
        if k == 0:
            idrecv[0] = picked
        else:
            idsend[k] = picked
            id_copy(k).start()

        def fill(j, carry):
            at = pl.ds(pl.multiple_of(j * width, width), width)
            block = jnp.dot(pick, hid[:, at], preferred_element_type=F32).astype(BF)
            if k == 0:
                for c in range(CHUNKS):
                    recv[c, 0, :, at] = block[c * step:(c + 1) * step]
            else:
                stage[k, :, at] = block
            return carry

        lax.fori_loop(0, feats // width, fill, 0)
        if k:
            row_copy(0, k).start()
            row_copy(1, k).start()

    loads[0].wait()
    tile = 256
    for k in list(range(1, m)) + [0]:
        at = pl.ds(pl.multiple_of(tp_of(k) * cols, cols), cols)

        def base(i, carry):
            rs = pl.ds(pl.multiple_of(i * tile, tile), tile)
            got = jnp.dot(hid[rs, :], wv[:, at], preferred_element_type=F32)
            if k == 0:
                fresh[rs, :] = got
            else:
                part[k, rs, :] = got.astype(BF)
            return carry

        lax.fori_loop(0, rows // tile, base, 0)
        if k:
            rs_copy(k).start()

    eye = lax.broadcasted_iota(jnp.int32, (cap, cap), 0) == lax.broadcasted_iota(
        jnp.int32, (cap, cap), 1
    )
    for k in range(n):
        if k:
            id_copy(k).wait()
        line = idrecv[k, 0:1, :].astype(F32)
        col = jnp.sum(jnp.where(eye, line, 0.0), axis=1, keepdims=True)
        col = jnp.broadcast_to(col, (cap, 128))
        for c in range(CHUNKS):
            idb[c, k * step:(k + 1) * step, :] = col[c * step:(c + 1) * step]

    for k in range(1, m):
        rs_copy(k).wait()
    loads[1].wait()
    loads[2].wait()

    lane = lax.broadcasted_iota(jnp.int32, (n * step, 128), 1)
    upper = jnp.where(lane < 64, 0.0, 1.0)
    halves = 2
    group = n // halves

    def chunk(c, carry):
        for k in range(1, n):
            row_copy(c, k).wait_send()

        @pl.when(c < CHUNKS - 2)
        def _():
            for k in far:
                row_copy(c + 2, k).start()

        for k in range(1, n):
            row_copy(c, k).wait_recv()
        for h in range(halves):
            block = recv[c, h * group:(h + 1) * group].reshape(group * step, feats)
            which = idb[c, h * group * step:(h + 1) * group * step, :]

            def pair(j, acc):
                both = jnp.concatenate([dv[2 * j], dv[2 * j + 1]], axis=1)
                got = jnp.dot(block, both, preferred_element_type=F32)
                first = (2 * j).astype(F32)
                acc = acc + jnp.where(which == first, got[:, :128], 0.0)
                return acc + jnp.where(which == first + 1.0, got[:, 128:], 0.0)

            acc = lax.fori_loop(
                0, adapters // 2, pair, jnp.zeros((group * step, 128), F32)
            )
            rkrecv[c, 0, h * group * step:(h + 1) * group * step, :] = acc.astype(BF)
            rkown[c, h * group * step:(h + 1) * group * step, :] = acc.astype(BF)
        for k in range(1, m):
            rank_copy(c, k).start()
        for k in range(1, m):
            rank_copy(c, k).wait()
        total = rkrecv[c, 0].astype(F32)
        for k in range(1, m):
            total = total + rkrecv[c, k].astype(F32)
        turned = pltpu.roll(total, 64, 1)
        keys = jnp.where(lane < 64, total, turned)
        vals = jnp.where(lane < 64, turned, total)
        which = idb[c]
        keys_by, vals_by = [], []
        for j in range(adapters // 2):
            mine = which == upper + float(2 * j)
            keys_by.append(jnp.where(mine, keys, 0.0).astype(BF))
            vals_by.append(jnp.where(mine, vals, 0.0).astype(BF))
        keys_by = jnp.concatenate(keys_by, axis=1)
        vals_by = jnp.concatenate(vals_by, axis=1)
        for b in range(cols // 128):
            mat = uv[:, b * 128:(b + 1) * 128]
            got = jnp.dot(
                keys_by if b % 2 == 0 else vals_by, mat, preferred_element_type=F32
            ).astype(BF)
            ret[c, 0, :, b * 128:(b + 1) * 128] = got[:step]
            for k in range(1, n):
                dout[c, k, :, b * 128:(b + 1) * 128] = got[k * step:(k + 1) * step]
        for k in far:
            delta_copy(c, k).start()
        return carry

    lax.fori_loop(0, CHUNKS, chunk, 0)

    starts = [start_of(dp_of(k)) for k in range(n)]
    for c in range(CHUNKS):
        for k in range(1, n):
            delta_copy(c, k).wait()

    def finish(i, carry):
        rs = pl.ds(pl.multiple_of(i * tile, tile), tile)
        total = fresh[rs, :]
        for k in range(1, m):
            total = total + rsrecv[k, rs, :].astype(F32)
        name = idc[rs, :]
        away = (
            lax.broadcasted_iota(jnp.int32, (tile, cap), 0)
            - lax.broadcasted_iota(jnp.int32, (tile, cap), 1)
            + i * tile
        ).astype(F32)
        for k in range(n):
            low = dp_of(k) * adapters
            mine = jnp.where((name >= low) & (name < low + adapters), 1.0, 0.0)
            put = jnp.where(away == starts[k], mine, 0.0).astype(BF)
            total = total + jnp.dot(
                put, ret[:, k].reshape(cap, cols), preferred_element_type=F32
            )
        fresh[rs, :] = total
        return carry

    lax.fori_loop(0, rows // tile, finish, 0)


def project(hid, ids, weight, down, up, n, m, cols, cap):
    rows, feats = hid.shape
    adapters = down.shape[0]
    step = cap // CHUNKS
    vm = pl.BlockSpec(memory_space=pltpu.VMEM)
    hbm = pl.BlockSpec(memory_space=pl.ANY)
    dma = pltpu.SemaphoreType.DMA
    return pl.pallas_call(
        functools.partial(project_kernel, n, m, adapters),
        out_shape=jax.ShapeDtypeStruct((rows, cols), F32),
        in_specs=[vm, vm, vm, hbm, hbm, hbm],
        out_specs=vm,
        scratch_shapes=[
            pltpu.VMEM(weight.shape, BF),
            pltpu.VMEM(down.shape, BF),
            pltpu.VMEM((adapters * up.shape[1], cols), BF),
            pltpu.VMEM((n, cap, feats), BF),
            pltpu.VMEM((CHUNKS, n, step, feats), BF),
            pltpu.VMEM((n, 16, cap), BF),
            pltpu.VMEM((n, 16, cap), BF),
            pltpu.VMEM((CHUNKS, n * step, 128), F32),
            pltpu.VMEM((m, rows, cols), BF),
            pltpu.VMEM((m, rows, cols), BF),
            pltpu.VMEM((CHUNKS, n * step, 128), BF),
            pltpu.VMEM((CHUNKS, m, n * step, 128), BF),
            pltpu.VMEM((CHUNKS, n, step, cols), BF),
            pltpu.VMEM((CHUNKS, n, step, cols), BF),
            dma((3,)),
            dma((CHUNKS, n)), dma((CHUNKS, n)),
            dma((n,)), dma((n,)),
            dma((m,)), dma((m,)),
            dma((CHUNKS, m)), dma((CHUNKS, m)),
            dma((CHUNKS, n)), dma((CHUNKS, n)),
        ],
        compiler_params=pltpu.CompilerParams(
            collective_id=0, has_side_effects=True, vmem_limit_bytes=62 * 1024 * 1024
        ),
        name="project",
    )(
        hid, jnp.broadcast_to(ids[None, :], (8, rows)), ids[:, None], weight, down,
        up.reshape(adapters * up.shape[1], cols),
    )


def attend_kernel(heads, slots, fresh, cosine, sine, bias, q, cache, new_kv, out):
    block = fresh.shape[0]
    span = 8
    grp = q.shape[2]
    dim = q.shape[3]
    scale = 1.0 / (dim ** 0.5)
    apart = jnp.where(
        lax.broadcasted_iota(jnp.int32, (span * grp, span * slots), 0) // grp
        == lax.broadcasted_iota(jnp.int32, (span * grp, span * slots), 1) // slots,
        0.0, BIG,
    )
    for h in range(heads):
        raw = fresh[:, (2 * h) * dim:(2 * h + 1) * dim]
        key = (raw * cosine[...] + pltpu.roll(raw, dim // 2, 1) * sine[...]).astype(BF)
        val = fresh[:, (2 * h + 1) * dim:(2 * h + 2) * dim].astype(BF)
        new_kv[0, h] = key
        new_kv[1, h] = val
        key = key.astype(F32)
        val = val.astype(F32)
        for s in range(block // span):
            at = slice(s * span, (s + 1) * span)
            qs = q[h, at].reshape(span * grp, dim)
            ks = cache[0, h, at].reshape(span * slots, dim)
            vs = cache[1, h, at].reshape(span * slots, dim)
            score = lax.dot_general(
                qs, ks, (((1,), (1,)), ((), ())), preferred_element_type=F32
            ) * scale + (apart + bias[0, s:s + 1, :])
            near = jnp.broadcast_to(key[at][:, None, :], (span, grp, dim))
            near = near.reshape(span * grp, dim)
            own = jnp.sum(qs.astype(F32) * near, axis=1, keepdims=True) * scale
            peak = jnp.maximum(jnp.max(score, axis=1, keepdims=True), own)
            probs = jnp.exp(score - peak)
            mine = jnp.exp(own - peak)
            total = jnp.sum(probs, axis=1, keepdims=True) + mine
            got = jnp.dot(probs.astype(BF), vs, preferred_element_type=F32)
            near = jnp.broadcast_to(val[at][:, None, :], (span, grp, dim))
            got = got + mine * near.reshape(span * grp, dim)
            got = got * (1.0 / total)
            out[h, at] = got.astype(BF).reshape(span, grp, dim)


def attend_all(fresh, queries, cache, lengths):
    heads, rows, grp, dim = queries.shape
    slots = cache.shape[3]
    block = 32
    span = 8
    inverse = rope_theta ** (-(2.0 * jnp.arange(dim // 2).astype(F32) / dim))
    angles = lengths[:, None].astype(F32) * inverse[None, :]
    cos, sin = jnp.cos(angles), jnp.sin(angles)
    cosine = jnp.concatenate([cos, cos], axis=1)
    sine = jnp.concatenate([-sin, sin], axis=1)
    live = jnp.arange(slots)[None, :] < lengths[:, None]
    bias = jnp.where(live, 0.0, BIG).astype(F32)
    bias = bias.reshape(rows // block, block // span, span * slots)
    return pl.pallas_call(
        functools.partial(attend_kernel, heads, slots),
        grid=(rows // block,),
        out_shape=(
            jax.ShapeDtypeStruct((2, heads, rows, dim), BF),
            jax.ShapeDtypeStruct(queries.shape, BF),
        ),
        in_specs=[
            pl.BlockSpec((block, fresh.shape[1]), lambda i: (i, 0)),
            pl.BlockSpec((block, dim), lambda i: (i, 0)),
            pl.BlockSpec((block, dim), lambda i: (i, 0)),
            pl.BlockSpec((1, block // span, span * slots), lambda i: (i, 0, 0)),
            pl.BlockSpec((heads, block, grp, dim), lambda i: (0, i, 0, 0)),
            pl.BlockSpec((2, heads, block, slots, dim), lambda i: (0, 0, i, 0, 0)),
        ],
        out_specs=(
            pl.BlockSpec((2, heads, block, dim), lambda i: (0, 0, i, 0)),
            pl.BlockSpec((heads, block, grp, dim), lambda i: (0, i, 0, 0)),
        ),
        compiler_params=pltpu.CompilerParams(vmem_limit_bytes=48 * 1024 * 1024),
        name="attend_all",
    )(fresh, cosine, sine, bias, queries, cache)


def fused_device(
    hidden_input, key_value_weight, adapter_down_weight, adapter_up_weight, queries,
    key_value_cache, request_adapter_index, cached_length,
):
    n, m = lax.axis_size("dp"), lax.axis_size("tensor")
    rows = hidden_input.shape[0]
    fresh = project(
        hidden_input, request_adapter_index, key_value_weight, adapter_down_weight,
        adapter_up_weight, n, m, adapter_up_weight.shape[2], 2 * rows // n,
    )
    return attend_all(fresh, queries, key_value_cache, cached_length)


def rotate_keys(key_rows, positions):
    head_size = key_rows.shape[-1]
    half_dim = head_size // 2
    freq_index = jnp.arange(half_dim).astype(key_rows.dtype)
    inverse = rope_theta ** (-(2.0 * freq_index / head_size))
    angles = positions[..., None].astype(key_rows.dtype) * inverse
    cosine = jnp.cos(angles)
    sine_part = jnp.sin(angles)
    first_half = key_rows[..., :half_dim]
    second_half = key_rows[..., half_dim:]
    return jnp.concatenate(
        [
            first_half * cosine - second_half * sine_part,
            second_half * cosine + first_half * sine_part,
        ],
        axis=-1,
    )


def attend(query_rows, cache_keys, cache_values, new_keys, new_values, lengths):
    score_scale = 1.0 / jnp.sqrt(jnp.float32(query_rows.shape[-1]))
    cache_scores = (
        jnp.einsum("igd,icd->igc", query_rows, cache_keys, preferred_element_type=jnp.float32)
        * score_scale
    )
    own_scores = (
        jnp.einsum("igd,id->ig", query_rows, new_keys, preferred_element_type=jnp.float32)
        * score_scale
    )
    valid_mask = (jnp.arange(cache_keys.shape[1])[None, :] < lengths[:, None])[:, None, :]
    masked = jnp.where(valid_mask, cache_scores, -1e30)
    peak_score = jnp.maximum(jnp.max(masked, axis=-1), own_scores)
    cache_exp = jnp.where(valid_mask, jnp.exp(masked - peak_score[..., None]), 0.0)
    own_exp = jnp.exp(own_scores - peak_score)
    denominator = jnp.sum(cache_exp, axis=-1) + own_exp
    cache_weights = (cache_exp / denominator[..., None]).astype(jnp.bfloat16)
    own_weights = (own_exp / denominator).astype(jnp.bfloat16)
    attended = jnp.einsum(
        "igc,icd->igd", cache_weights, cache_values, preferred_element_type=jnp.float32
    )
    attended = (
        attended
        + own_weights.astype(jnp.float32)[..., None] * new_values.astype(jnp.float32)[:, None, :]
    )
    return attended.astype(jnp.bfloat16)


def per_device(
    hidden_input,
    key_value_weight,
    adapter_down_weight,
    adapter_up_weight,
    queries,
    key_value_cache,
    request_adapter_index,
    cached_length,
):
    row_count, feat_count = hidden_input.shape
    owner_count = lax.axis_size("dp")
    adapter_total = adapter_down_weight.shape[0]
    adapter_rank_width = adapter_down_weight.shape[2] // 2
    column_extent = adapter_up_weight.shape[2]
    head_dim = queries.shape[3]
    heads_here = queries.shape[0]
    rows_here = queries.shape[1]
    split_count = row_count // rows_here
    if split_count == 1 and column_extent == 2 * head_dim * heads_here and head_dim == 128:
        return fused_device(
            hidden_input, key_value_weight, adapter_down_weight, adapter_up_weight,
            queries, key_value_cache, request_adapter_index, cached_length,
        )
    capacity = 2 * row_count // owner_count
    kv_heads = key_value_weight.shape[1] // (2 * head_dim)
    tensor_index = lax.axis_index("tensor")
    owner_of = request_adapter_index // adapter_total
    owner_match = (owner_of[:, None] == jnp.arange(owner_count)[None, :]).astype(jnp.int32)
    counts = jnp.sum(owner_match, axis=0)
    before = jnp.arange(owner_count)[None, :] < jnp.arange(owner_count)[:, None]
    starts = jnp.sum(jnp.where(before, counts[None, :], 0), axis=1)
    slot_rows = starts[:, None] + jnp.arange(capacity)[None, :]
    padded_rows = jnp.concatenate(
        [hidden_input, jnp.zeros((capacity, feat_count), hidden_input.dtype)], axis=0
    )
    local_ids = request_adapter_index - owner_of * adapter_total
    padded_ids = jnp.concatenate([local_ids, jnp.zeros((capacity,), jnp.int32)])
    slot_live = jnp.arange(capacity)[None, :] < counts[:, None]
    send_rows = jnp.take(padded_rows, slot_rows, axis=0)
    send_ids = jnp.where(slot_live, jnp.take(padded_ids, slot_rows, axis=0), -1).astype(
        jnp.bfloat16
    )
    column_piece = (tensor_index * column_extent + jnp.arange(column_extent)) // head_dim
    key_columns = column_piece % 2 == 0
    raised_flattened = adapter_up_weight.reshape(adapter_total * adapter_rank_width, column_extent)
    rows_in = lax.all_to_all(send_rows, "dp", split_axis=0, concat_axis=0, tiled=True)
    ids_in = lax.all_to_all(send_ids, "dp", split_axis=0, concat_axis=0, tiled=True)
    sources, item_count = ids_in.shape
    flattened_rows = rows_in.reshape(sources * item_count, feat_count)
    flat_ids = ids_in.reshape(sources * item_count)
    one_hot = (flat_ids[:, None] == jnp.arange(adapter_total).astype(jnp.bfloat16)[None, :]).astype(
        jnp.bfloat16
    )
    matrix_products = jnp.einsum(
        "nt,wtz->nwz", flattened_rows, adapter_down_weight, preferred_element_type=jnp.float32
    )
    partial_rank = jnp.sum(matrix_products * one_hot[:, :, None], axis=1)
    full_rank = lax.psum(partial_rank, "tensor").astype(jnp.bfloat16)
    chosen = one_hot[:, :, None] * full_rank[:, None, :]
    key_rank = chosen[:, :, :adapter_rank_width].reshape(
        sources * item_count, adapter_total * adapter_rank_width
    )
    value_rank = chosen[:, :, adapter_rank_width:].reshape(
        sources * item_count, adapter_total * adapter_rank_width
    )
    key_delta = jnp.dot(key_rank, raised_flattened, preferred_element_type=jnp.float32)
    value_delta = jnp.dot(value_rank, raised_flattened, preferred_element_type=jnp.float32)
    delta_cols = jnp.where(key_columns[None, :], key_delta, value_delta).astype(jnp.bfloat16)
    delta_cols = delta_cols.reshape(sources, item_count, column_extent)
    returned = lax.all_to_all(delta_cols, "dp", split_axis=0, concat_axis=0, tiled=True)
    slot_index = owner_of * capacity + (jnp.arange(row_count) - jnp.take(starts, owner_of))
    delta_rows = jnp.take(
        returned.reshape(owner_count * capacity, column_extent), slot_index, axis=0
    )
    base_sum = jnp.dot(hidden_input, key_value_weight, preferred_element_type=jnp.float32)
    column_start = tensor_index * column_extent
    own_columns = lax.dynamic_slice_in_dim(
        base_sum, column_start, column_extent, 1
    ) + delta_rows.astype(jnp.float32)
    partial_value = lax.dynamic_update_slice_in_dim(base_sum, own_columns, column_start, 1)
    first_row = tensor_index * heads_here
    half_index = first_row % split_count
    head_start = first_row // split_count
    head_span = (heads_here + split_count - 1) // split_count
    summed = lax.psum(partial_value, "tensor")
    summed_view = summed.reshape(split_count, rows_here, kv_heads, 2, head_dim)
    own_part = lax.dynamic_slice(
        summed_view, (half_index, 0, head_start, 0, 0), (1, rows_here, head_span, 2, head_dim)
    )[0]
    fresh_kv = jnp.transpose(own_part, (2, 1, 0, 3))
    lens_here = lax.dynamic_slice_in_dim(cached_length, half_index * rows_here, rows_here, 0)
    new_keys = rotate_keys(fresh_kv[0], lens_here[None, :])
    new_kv = jnp.stack([new_keys, fresh_kv[1]]).astype(jnp.bfloat16)
    flat_count = heads_here * rows_here
    cache_slots = key_value_cache.shape[3]
    attn_out = attend(
        queries.reshape(flat_count, queries.shape[2], head_dim),
        key_value_cache[0].reshape(flat_count, cache_slots, head_dim),
        key_value_cache[1].reshape(flat_count, cache_slots, head_dim),
        new_kv[0].reshape(flat_count, head_dim),
        new_kv[1].reshape(flat_count, head_dim),
        jnp.tile(lens_here, heads_here),
    ).reshape(queries.shape)
    return (new_kv, attn_out)


def solution(mesh):
    return jax.shard_map(
        per_device,
        mesh=mesh,
        in_specs=(
            P("dp", "tensor"),
            P("tensor", None),
            P("dp", "tensor", None),
            P("dp", None, "tensor"),
            P("tensor", "dp", None, None),
            P(None, "tensor", "dp", None, None),
            P("dp"),
            P("dp"),
        ),
        out_specs=(P(None, "tensor", "dp", None), P("tensor", "dp", None, None)),
        check_vma=False,
    )
```

```python
import functools

import jax
import jax.numpy as jnp
from jax import lax
from jax.experimental import pallas as pl
from jax.experimental.pallas import tpu as pltpu
from jax.sharding import PartitionSpec as P

rope_theta = 500000.0
MESH = pl.DeviceIdType.MESH
BF = jnp.bfloat16
F32 = jnp.float32
CHUNKS = 4
BIG = -1e30


def project_kernel(
    n, m, adapters, hid, idr, idc, w_hbm, dn_hbm, up_hbm, fresh,
    wv, dv, uv, stage, recv, idsend, idrecv, idb, part, rsrecv, rkown, rkrecv, dout, ret,
    load_sem, row_s, row_r, id_s, id_r, rs_s, rs_r, rk_s, rk_r, dl_s, dl_r,
):
    me = lax.axis_index("dp")
    mt = lax.axis_index("tensor")
    rows, feats = hid.shape
    cap = stage.shape[1]
    step = cap // CHUNKS
    cols = fresh.shape[1]
    far = sorted(range(1, n), key=lambda k: (abs(k - n // 2), k))

    def dp_of(k):
        return lax.rem(me + k + n, n)

    def tp_of(k):
        return lax.rem(mt + k + m, m)

    barrier = pltpu.get_barrier_semaphore()
    for k in range(1, n):
        pl.semaphore_signal(barrier, inc=1, device_id=(dp_of(k), mt), device_id_type=MESH)
    for k in range(1, m):
        pl.semaphore_signal(barrier, inc=1, device_id=(me, tp_of(k)), device_id_type=MESH)
    loads = [
        pltpu.make_async_copy(w_hbm, wv, load_sem.at[0]),
        pltpu.make_async_copy(dn_hbm, dv, load_sem.at[1]),
        pltpu.make_async_copy(up_hbm, uv, load_sem.at[2]),
    ]
    for load in loads:
        load.start()
    pl.semaphore_wait(barrier, n - 1 + m - 1)

    def row_copy(c, k):
        return pltpu.make_async_remote_copy(
            src_ref=stage.at[k, pl.ds(pl.multiple_of(c * step, step), step)],
            dst_ref=recv.at[c, k],
            send_sem=row_s.at[c, k], recv_sem=row_r.at[c, k],
            device_id=(dp_of(k), mt), device_id_type=MESH,
        )

    def id_copy(k):
        return pltpu.make_async_remote_copy(
            src_ref=idsend.at[k], dst_ref=idrecv.at[k],
            send_sem=id_s.at[k], recv_sem=id_r.at[k],
            device_id=(dp_of(k), mt), device_id_type=MESH,
        )

    def rs_copy(k):
        return pltpu.make_async_remote_copy(
            src_ref=part.at[k], dst_ref=rsrecv.at[k],
            send_sem=rs_s.at[k], recv_sem=rs_r.at[k],
            device_id=(me, tp_of(k)), device_id_type=MESH,
        )

    def rank_copy(c, k):
        return pltpu.make_async_remote_copy(
            src_ref=rkown.at[c], dst_ref=rkrecv.at[c, k],
            send_sem=rk_s.at[c, k], recv_sem=rk_r.at[c, k],
            device_id=(me, tp_of(k)), device_id_type=MESH,
        )

    def delta_copy(c, k):
        return pltpu.make_async_remote_copy(
            src_ref=dout.at[c, k], dst_ref=ret.at[c, k],
            send_sem=dl_s.at[c, k], recv_sem=dl_r.at[c, k],
            device_id=(dp_of(-k), mt), device_id_type=MESH,
        )

    ids_row = idr[0:1, :]

    def start_of(owner):
        below = jnp.where(ids_row < owner * adapters, 1.0, 0.0)
        return jnp.minimum(jnp.sum(below, axis=1, keepdims=True), float(rows - cap))

    gap = (
        lax.broadcasted_iota(jnp.int32, (cap, rows), 1)
        - lax.broadcasted_iota(jnp.int32, (cap, rows), 0)
    ).astype(F32)
    width = 512
    for k in far + [0]:
        owner = dp_of(k)
        pick = jnp.where(gap == start_of(owner), 1.0, 0.0).astype(BF)
        local = (ids_row - owner * adapters).astype(F32)
        local = jnp.broadcast_to(local, (16, rows)).astype(BF)
        picked = lax.dot_general(
            local, pick, (((1,), (1,)), ((), ())), preferred_element_type=F32
        ).astype(BF)
        if k == 0:
            idrecv[0] = picked
        else:
            idsend[k] = picked
            id_copy(k).start()

        def fill(j, carry):
            at = pl.ds(pl.multiple_of(j * width, width), width)
            block = jnp.dot(pick, hid[:, at], preferred_element_type=F32).astype(BF)
            if k == 0:
                for c in range(CHUNKS):
                    recv[c, 0, :, at] = block[c * step:(c + 1) * step]
            else:
                stage[k, :, at] = block
            return carry

        lax.fori_loop(0, feats // width, fill, 0)
        if k:
            row_copy(0, k).start()
            row_copy(1, k).start()

    loads[0].wait()
    tile = 256
    for k in list(range(1, m)) + [0]:
        at = pl.ds(pl.multiple_of(tp_of(k) * cols, cols), cols)

        def base(i, carry):
            rs = pl.ds(pl.multiple_of(i * tile, tile), tile)
            got = jnp.dot(hid[rs, :], wv[:, at], preferred_element_type=F32)
            if k == 0:
                fresh[rs, :] = got
            else:
                part[k, rs, :] = got.astype(BF)
            return carry

        lax.fori_loop(0, rows // tile, base, 0)
        if k:
            rs_copy(k).start()

    eye = lax.broadcasted_iota(jnp.int32, (cap, cap), 0) == lax.broadcasted_iota(
        jnp.int32, (cap, cap), 1
    )
    for k in range(n):
        if k:
            id_copy(k).wait()
        line = idrecv[k, 0:1, :].astype(F32)
        col = jnp.sum(jnp.where(eye, line, 0.0), axis=1, keepdims=True)
        col = jnp.broadcast_to(col, (cap, 128))
        for c in range(CHUNKS):
            idb[c, k * step:(k + 1) * step, :] = col[c * step:(c + 1) * step]

    for k in range(1, m):
        rs_copy(k).wait()
    loads[1].wait()
    loads[2].wait()

    lane = lax.broadcasted_iota(jnp.int32, (n * step, 128), 1)
    upper = jnp.where(lane < 64, 0.0, 1.0)
    halves = 2
    group = n // halves

    def chunk(c, carry):
        for k in range(1, n):
            row_copy(c, k).wait_send()

        @pl.when(c < CHUNKS - 2)
        def _():
            for k in far:
                row_copy(c + 2, k).start()

        for k in range(1, n):
            row_copy(c, k).wait_recv()
        for h in range(halves):
            block = recv[c, h * group:(h + 1) * group].reshape(group * step, feats)
            which = idb[c, h * group * step:(h + 1) * group * step, :]

            def pair(j, acc):
                both = jnp.concatenate([dv[2 * j], dv[2 * j + 1]], axis=1)
                got = jnp.dot(block, both, preferred_element_type=F32)
                first = (2 * j).astype(F32)
                acc = acc + jnp.where(which == first, got[:, :128], 0.0)
                return acc + jnp.where(which == first + 1.0, got[:, 128:], 0.0)

            acc = lax.fori_loop(
                0, adapters // 2, pair, jnp.zeros((group * step, 128), F32)
            )
            rkrecv[c, 0, h * group * step:(h + 1) * group * step, :] = acc.astype(BF)
            rkown[c, h * group * step:(h + 1) * group * step, :] = acc.astype(BF)
        for k in range(1, m):
            rank_copy(c, k).start()
        for k in range(1, m):
            rank_copy(c, k).wait()
        total = rkrecv[c, 0].astype(F32)
        for k in range(1, m):
            total = total + rkrecv[c, k].astype(F32)
        turned = pltpu.roll(total, 64, 1)
        keys = jnp.where(lane < 64, total, turned)
        vals = jnp.where(lane < 64, turned, total)
        which = idb[c]
        keys_by, vals_by = [], []
        for j in range(adapters // 2):
            mine = which == upper + float(2 * j)
            keys_by.append(jnp.where(mine, keys, 0.0).astype(BF))
            vals_by.append(jnp.where(mine, vals, 0.0).astype(BF))
        keys_by = jnp.concatenate(keys_by, axis=1)
        vals_by = jnp.concatenate(vals_by, axis=1)
        for b in range(cols // 128):
            mat = uv[:, b * 128:(b + 1) * 128]
            got = jnp.dot(
                keys_by if b % 2 == 0 else vals_by, mat, preferred_element_type=F32
            ).astype(BF)
            ret[c, 0, :, b * 128:(b + 1) * 128] = got[:step]
            for k in range(1, n):
                dout[c, k, :, b * 128:(b + 1) * 128] = got[k * step:(k + 1) * step]
        for k in far:
            delta_copy(c, k).start()
        return carry

    lax.fori_loop(0, CHUNKS, chunk, 0)

    starts = [start_of(dp_of(k)) for k in range(n)]
    for c in range(CHUNKS):
        for k in range(1, n):
            delta_copy(c, k).wait()

    def finish(i, carry):
        rs = pl.ds(pl.multiple_of(i * tile, tile), tile)
        total = fresh[rs, :]
        for k in range(1, m):
            total = total + rsrecv[k, rs, :].astype(F32)
        name = idc[rs, :]
        away = (
            lax.broadcasted_iota(jnp.int32, (tile, cap), 0)
            - lax.broadcasted_iota(jnp.int32, (tile, cap), 1)
            + i * tile
        ).astype(F32)
        for k in range(n):
            low = dp_of(k) * adapters
            mine = jnp.where((name >= low) & (name < low + adapters), 1.0, 0.0)
            put = jnp.where(away == starts[k], mine, 0.0).astype(BF)
            total = total + jnp.dot(
                put, ret[:, k].reshape(cap, cols), preferred_element_type=F32
            )
        fresh[rs, :] = total
        return carry

    lax.fori_loop(0, rows // tile, finish, 0)


def project(hid, ids, weight, down, up, n, m, cols, cap):
    rows, feats = hid.shape
    adapters = down.shape[0]
    step = cap // CHUNKS
    vm = pl.BlockSpec(memory_space=pltpu.VMEM)
    hbm = pl.BlockSpec(memory_space=pl.ANY)
    dma = pltpu.SemaphoreType.DMA
    return pl.pallas_call(
        functools.partial(project_kernel, n, m, adapters),
        out_shape=jax.ShapeDtypeStruct((rows, cols), F32),
        in_specs=[vm, vm, vm, hbm, hbm, hbm],
        out_specs=vm,
        scratch_shapes=[
            pltpu.VMEM(weight.shape, BF),
            pltpu.VMEM(down.shape, BF),
            pltpu.VMEM((adapters * up.shape[1], cols), BF),
            pltpu.VMEM((n, cap, feats), BF),
            pltpu.VMEM((CHUNKS, n, step, feats), BF),
            pltpu.VMEM((n, 16, cap), BF),
            pltpu.VMEM((n, 16, cap), BF),
            pltpu.VMEM((CHUNKS, n * step, 128), F32),
            pltpu.VMEM((m, rows, cols), BF),
            pltpu.VMEM((m, rows, cols), BF),
            pltpu.VMEM((CHUNKS, n * step, 128), BF),
            pltpu.VMEM((CHUNKS, m, n * step, 128), BF),
            pltpu.VMEM((CHUNKS, n, step, cols), BF),
            pltpu.VMEM((CHUNKS, n, step, cols), BF),
            dma((3,)),
            dma((CHUNKS, n)), dma((CHUNKS, n)),
            dma((n,)), dma((n,)),
            dma((m,)), dma((m,)),
            dma((CHUNKS, m)), dma((CHUNKS, m)),
            dma((CHUNKS, n)), dma((CHUNKS, n)),
        ],
        compiler_params=pltpu.CompilerParams(
            collective_id=0, has_side_effects=True, vmem_limit_bytes=62 * 1024 * 1024
        ),
        name="project",
    )(
        hid, jnp.broadcast_to(ids[None, :], (8, rows)), ids[:, None], weight, down,
        up.reshape(adapters * up.shape[1], cols),
    )


def attend_kernel(heads, slots, fresh, cosine, sine, bias, q, cache, new_kv, out):
    block = fresh.shape[0]
    span = 8
    grp = q.shape[2]
    dim = q.shape[3]
    scale = 1.0 / (dim ** 0.5)
    apart = jnp.where(
        lax.broadcasted_iota(jnp.int32, (span * grp, span * slots), 0) // grp
        == lax.broadcasted_iota(jnp.int32, (span * grp, span * slots), 1) // slots,
        0.0, BIG,
    )
    for h in range(heads):
        raw = fresh[:, (2 * h) * dim:(2 * h + 1) * dim]
        key = (raw * cosine[...] + pltpu.roll(raw, dim // 2, 1) * sine[...]).astype(BF)
        val = fresh[:, (2 * h + 1) * dim:(2 * h + 2) * dim].astype(BF)
        new_kv[0, h] = key
        new_kv[1, h] = val
        key = key.astype(F32)
        val = val.astype(F32)
        for first in range(0, block // span, 4):
            spans = [slice((first + s) * span, (first + s + 1) * span) for s in range(4)]
            qs = [q[h, at].reshape(span * grp, dim) for at in spans]
            scores = [
                lax.dot_general(
                    qs[s], cache[0, h, spans[s]].reshape(span * slots, dim),
                    (((1,), (1,)), ((), ())), preferred_element_type=F32,
                )
                for s in range(4)
            ]
            near = [
                jnp.broadcast_to(key[at][:, None, :], (span, grp, dim)).reshape(span * grp, dim)
                for at in spans
            ]
            own = [
                jnp.sum(qs[s].astype(F32) * near[s], axis=1, keepdims=True) * scale
                for s in range(4)
            ]
            scores = [
                scores[s] * scale + (apart + bias[0, first + s:first + s + 1, :])
                for s in range(4)
            ]
            peaks = [
                jnp.maximum(jnp.max(scores[s], axis=1, keepdims=True), own[s]) for s in range(4)
            ]
            probs = [jnp.exp(scores[s] - peaks[s]) for s in range(4)]
            mine = [jnp.exp(own[s] - peaks[s]) for s in range(4)]
            totals = [jnp.sum(probs[s], axis=1, keepdims=True) + mine[s] for s in range(4)]
            got = [
                jnp.dot(
                    probs[s].astype(BF), cache[1, h, spans[s]].reshape(span * slots, dim),
                    preferred_element_type=F32,
                )
                for s in range(4)
            ]
            for s in range(4):
                near = jnp.broadcast_to(val[spans[s]][:, None, :], (span, grp, dim))
                full = got[s] + mine[s] * near.reshape(span * grp, dim)
                full = full * (1.0 / totals[s])
                out[h, spans[s]] = full.astype(BF).reshape(span, grp, dim)


def attend_all(fresh, queries, cache, lengths):
    heads, rows, grp, dim = queries.shape
    slots = cache.shape[3]
    block = 64
    span = 8
    inverse = rope_theta ** (-(2.0 * jnp.arange(dim // 2).astype(F32) / dim))
    angles = lengths[:, None].astype(F32) * inverse[None, :]
    cos, sin = jnp.cos(angles), jnp.sin(angles)
    cosine = jnp.concatenate([cos, cos], axis=1)
    sine = jnp.concatenate([-sin, sin], axis=1)
    live = jnp.arange(slots)[None, :] < lengths[:, None]
    bias = jnp.where(live, 0.0, BIG).astype(F32)
    bias = bias.reshape(rows // block, block // span, span * slots)
    return pl.pallas_call(
        functools.partial(attend_kernel, heads, slots),
        grid=(rows // block,),
        out_shape=(
            jax.ShapeDtypeStruct((2, heads, rows, dim), BF),
            jax.ShapeDtypeStruct(queries.shape, BF),
        ),
        in_specs=[
            pl.BlockSpec((block, fresh.shape[1]), lambda i: (i, 0)),
            pl.BlockSpec((block, dim), lambda i: (i, 0)),
            pl.BlockSpec((block, dim), lambda i: (i, 0)),
            pl.BlockSpec((1, block // span, span * slots), lambda i: (i, 0, 0)),
            pl.BlockSpec((heads, block, grp, dim), lambda i: (0, i, 0, 0)),
            pl.BlockSpec((2, heads, block, slots, dim), lambda i: (0, 0, i, 0, 0)),
        ],
        out_specs=(
            pl.BlockSpec((2, heads, block, dim), lambda i: (0, 0, i, 0)),
            pl.BlockSpec((heads, block, grp, dim), lambda i: (0, i, 0, 0)),
        ),
        compiler_params=pltpu.CompilerParams(vmem_limit_bytes=48 * 1024 * 1024),
        name="attend_all",
    )(fresh, cosine, sine, bias, queries, cache)


def fused_device(
    hidden_input, key_value_weight, adapter_down_weight, adapter_up_weight, queries,
    key_value_cache, request_adapter_index, cached_length,
):
    n, m = lax.axis_size("dp"), lax.axis_size("tensor")
    rows = hidden_input.shape[0]
    fresh = project(
        hidden_input, request_adapter_index, key_value_weight, adapter_down_weight,
        adapter_up_weight, n, m, adapter_up_weight.shape[2], 2 * rows // n,
    )
    return attend_all(fresh, queries, key_value_cache, cached_length)


def rotate_keys(key_rows, positions):
    head_size = key_rows.shape[-1]
    half_dim = head_size // 2
    freq_index = jnp.arange(half_dim).astype(key_rows.dtype)
    inverse = rope_theta ** (-(2.0 * freq_index / head_size))
    angles = positions[..., None].astype(key_rows.dtype) * inverse
    cosine = jnp.cos(angles)
    sine_part = jnp.sin(angles)
    first_half = key_rows[..., :half_dim]
    second_half = key_rows[..., half_dim:]
    return jnp.concatenate(
        [
            first_half * cosine - second_half * sine_part,
            second_half * cosine + first_half * sine_part,
        ],
        axis=-1,
    )


def attend(query_rows, cache_keys, cache_values, new_keys, new_values, lengths):
    score_scale = 1.0 / jnp.sqrt(jnp.float32(query_rows.shape[-1]))
    cache_scores = (
        jnp.einsum("igd,icd->igc", query_rows, cache_keys, preferred_element_type=jnp.float32)
        * score_scale
    )
    own_scores = (
        jnp.einsum("igd,id->ig", query_rows, new_keys, preferred_element_type=jnp.float32)
        * score_scale
    )
    valid_mask = (jnp.arange(cache_keys.shape[1])[None, :] < lengths[:, None])[:, None, :]
    masked = jnp.where(valid_mask, cache_scores, -1e30)
    peak_score = jnp.maximum(jnp.max(masked, axis=-1), own_scores)
    cache_exp = jnp.where(valid_mask, jnp.exp(masked - peak_score[..., None]), 0.0)
    own_exp = jnp.exp(own_scores - peak_score)
    denominator = jnp.sum(cache_exp, axis=-1) + own_exp
    cache_weights = (cache_exp / denominator[..., None]).astype(jnp.bfloat16)
    own_weights = (own_exp / denominator).astype(jnp.bfloat16)
    attended = jnp.einsum(
        "igc,icd->igd", cache_weights, cache_values, preferred_element_type=jnp.float32
    )
    attended = (
        attended
        + own_weights.astype(jnp.float32)[..., None] * new_values.astype(jnp.float32)[:, None, :]
    )
    return attended.astype(jnp.bfloat16)


def per_device(
    hidden_input,
    key_value_weight,
    adapter_down_weight,
    adapter_up_weight,
    queries,
    key_value_cache,
    request_adapter_index,
    cached_length,
):
    row_count, feat_count = hidden_input.shape
    owner_count = lax.axis_size("dp")
    adapter_total = adapter_down_weight.shape[0]
    adapter_rank_width = adapter_down_weight.shape[2] // 2
    column_extent = adapter_up_weight.shape[2]
    head_dim = queries.shape[3]
    heads_here = queries.shape[0]
    rows_here = queries.shape[1]
    split_count = row_count // rows_here
    if split_count == 1 and column_extent == 2 * head_dim * heads_here and head_dim == 128:
        return fused_device(
            hidden_input, key_value_weight, adapter_down_weight, adapter_up_weight,
            queries, key_value_cache, request_adapter_index, cached_length,
        )
    capacity = 2 * row_count // owner_count
    kv_heads = key_value_weight.shape[1] // (2 * head_dim)
    tensor_index = lax.axis_index("tensor")
    owner_of = request_adapter_index // adapter_total
    owner_match = (owner_of[:, None] == jnp.arange(owner_count)[None, :]).astype(jnp.int32)
    counts = jnp.sum(owner_match, axis=0)
    before = jnp.arange(owner_count)[None, :] < jnp.arange(owner_count)[:, None]
    starts = jnp.sum(jnp.where(before, counts[None, :], 0), axis=1)
    slot_rows = starts[:, None] + jnp.arange(capacity)[None, :]
    padded_rows = jnp.concatenate(
        [hidden_input, jnp.zeros((capacity, feat_count), hidden_input.dtype)], axis=0
    )
    local_ids = request_adapter_index - owner_of * adapter_total
    padded_ids = jnp.concatenate([local_ids, jnp.zeros((capacity,), jnp.int32)])
    slot_live = jnp.arange(capacity)[None, :] < counts[:, None]
    send_rows = jnp.take(padded_rows, slot_rows, axis=0)
    send_ids = jnp.where(slot_live, jnp.take(padded_ids, slot_rows, axis=0), -1).astype(
        jnp.bfloat16
    )
    column_piece = (tensor_index * column_extent + jnp.arange(column_extent)) // head_dim
    key_columns = column_piece % 2 == 0
    raised_flattened = adapter_up_weight.reshape(adapter_total * adapter_rank_width, column_extent)
    rows_in = lax.all_to_all(send_rows, "dp", split_axis=0, concat_axis=0, tiled=True)
    ids_in = lax.all_to_all(send_ids, "dp", split_axis=0, concat_axis=0, tiled=True)
    sources, item_count = ids_in.shape
    flattened_rows = rows_in.reshape(sources * item_count, feat_count)
    flat_ids = ids_in.reshape(sources * item_count)
    one_hot = (flat_ids[:, None] == jnp.arange(adapter_total).astype(jnp.bfloat16)[None, :]).astype(
        jnp.bfloat16
    )
    matrix_products = jnp.einsum(
        "nt,wtz->nwz", flattened_rows, adapter_down_weight, preferred_element_type=jnp.float32
    )
    partial_rank = jnp.sum(matrix_products * one_hot[:, :, None], axis=1)
    full_rank = lax.psum(partial_rank, "tensor").astype(jnp.bfloat16)
    chosen = one_hot[:, :, None] * full_rank[:, None, :]
    key_rank = chosen[:, :, :adapter_rank_width].reshape(
        sources * item_count, adapter_total * adapter_rank_width
    )
    value_rank = chosen[:, :, adapter_rank_width:].reshape(
        sources * item_count, adapter_total * adapter_rank_width
    )
    key_delta = jnp.dot(key_rank, raised_flattened, preferred_element_type=jnp.float32)
    value_delta = jnp.dot(value_rank, raised_flattened, preferred_element_type=jnp.float32)
    delta_cols = jnp.where(key_columns[None, :], key_delta, value_delta).astype(jnp.bfloat16)
    delta_cols = delta_cols.reshape(sources, item_count, column_extent)
    returned = lax.all_to_all(delta_cols, "dp", split_axis=0, concat_axis=0, tiled=True)
    slot_index = owner_of * capacity + (jnp.arange(row_count) - jnp.take(starts, owner_of))
    delta_rows = jnp.take(
        returned.reshape(owner_count * capacity, column_extent), slot_index, axis=0
    )
    base_sum = jnp.dot(hidden_input, key_value_weight, preferred_element_type=jnp.float32)
    column_start = tensor_index * column_extent
    own_columns = lax.dynamic_slice_in_dim(
        base_sum, column_start, column_extent, 1
    ) + delta_rows.astype(jnp.float32)
    partial_value = lax.dynamic_update_slice_in_dim(base_sum, own_columns, column_start, 1)
    first_row = tensor_index * heads_here
    half_index = first_row % split_count
    head_start = first_row // split_count
    head_span = (heads_here + split_count - 1) // split_count
    summed = lax.psum(partial_value, "tensor")
    summed_view = summed.reshape(split_count, rows_here, kv_heads, 2, head_dim)
    own_part = lax.dynamic_slice(
        summed_view, (half_index, 0, head_start, 0, 0), (1, rows_here, head_span, 2, head_dim)
    )[0]
    fresh_kv = jnp.transpose(own_part, (2, 1, 0, 3))
    lens_here = lax.dynamic_slice_in_dim(cached_length, half_index * rows_here, rows_here, 0)
    new_keys = rotate_keys(fresh_kv[0], lens_here[None, :])
    new_kv = jnp.stack([new_keys, fresh_kv[1]]).astype(jnp.bfloat16)
    flat_count = heads_here * rows_here
    cache_slots = key_value_cache.shape[3]
    attn_out = attend(
        queries.reshape(flat_count, queries.shape[2], head_dim),
        key_value_cache[0].reshape(flat_count, cache_slots, head_dim),
        key_value_cache[1].reshape(flat_count, cache_slots, head_dim),
        new_kv[0].reshape(flat_count, head_dim),
        new_kv[1].reshape(flat_count, head_dim),
        jnp.tile(lens_here, heads_here),
    ).reshape(queries.shape)
    return (new_kv, attn_out)


def solution(mesh):
    return jax.shard_map(
        per_device,
        mesh=mesh,
        in_specs=(
            P("dp", "tensor"),
            P("tensor", None),
            P("dp", "tensor", None),
            P("dp", None, "tensor"),
            P("tensor", "dp", None, None),
            P(None, "tensor", "dp", None, None),
            P("dp"),
            P("dp"),
        ),
        out_specs=(P(None, "tensor", "dp", None), P("tensor", "dp", None, None)),
        check_vma=False,
    )
```
